256 devices in a mesh: row: 16 (over z, x_hi), col: 8 (over y, core), wa: 2 (over x_lo).
Axes of the slice: x: 4 (x_hi: 2, x_lo: 2; x = x_hi * 2 + x_lo), y: 4, z: 8, core: 2. Of those that a mesh axis runs over, the one named last changes fastest.
Arguments:
- iterate: bfloat16 [8192, 9216], P(('wa', 'row'), 'col'), parts along dimension 0, may hold values from -3.59375 to 3.59375
Outputs:
- next_iterate: bfloat16 [8192, 9216], P(('wa', 'row'), 'col'), parts along dimension 0
The draws below stay inside these ranges and needn't reach their ends.
There are 2 independent parts, one for each index of `wa`. The reference program is written for one: setup_inputs(seed, part) draws one part's arguments, and reference() takes and returns one part's arrays. A program takes and returns all parts, laid end to end along the dimension named above; each array names one. Nothing has to cross between parts.
All inputs are finite; a program needn't handle non-finite values.
Results may differ from the reference program's by a relative error of at most 0.0053.
Values may be sent and summed in bfloat16 or wider, within the bound.
No kernel may reach another device: no remote copies, remote signals or barrier semaphores. Data moves between devices by JAX's collectives and lax.ppermute only.
A program may use at most 64 MiB of HBM per device.

```python
import jax
import jax.numpy as jnp
from jax import lax

M = 4096
N = 9216


def level_of(key, shape, cuts, low, largest):
    level, own = 1.0, jax.random.fold_in(key, 6)
    for axis_at, blocks in cuts:
        steps = jnp.exp(jax.random.uniform(jax.random.fold_in(own, axis_at), (blocks,), jnp.float32, low / len(cuts), largest / len(cuts)))
        level = level * jnp.repeat(steps, shape[axis_at] // blocks).reshape([-1 if axis == axis_at else 1 for axis in range(len(shape))])
    return level


def scatter_about(key, shape, deviation, most, split=(), kind=jnp.bfloat16):
    entries = deviation * jax.random.normal(key, shape, jnp.float32)
    if split:
        entries = entries * level_of(key, shape, split, -0.22, 0.18)
    return jnp.clip(entries, -most, most).astype(kind)


def setup_inputs(seed: int = 0, part: int = 0) -> dict:
    arg_keys = jax.random.split(jax.random.key(seed), 2)
    part_keys = jax.random.split(jax.random.fold_in(arg_keys[1], part), 2)
    return {
        "iterate": scatter_about(part_keys[0], (M, N), 0.6, 3.59375, ((0, 16), (1, 8))),
    }


coef_first = 3.4445
coef_second = -4.7750
coef_third = 2.0315


def reference(iterate):
    gram = lax.dot_general(iterate, iterate, (((1,), (1,)), ((), ())), preferred_element_type=jnp.float32)
    gram_half = (gram / N).astype(jnp.bfloat16)
    square = jnp.dot(gram_half, gram_half, preferred_element_type=jnp.float32)
    poly = (coef_second * gram_half.astype(jnp.float32) + coef_third * square).astype(jnp.bfloat16)
    applied = jnp.dot(poly, iterate, preferred_element_type=jnp.float32)
    return (coef_first * iterate.astype(jnp.float32) + applied).astype(jnp.bfloat16)
```

```python
import jax
import jax.numpy as jnp
from jax import lax
from jax.sharding import PartitionSpec as P

coef_first = 3.4445
coef_second = -4.775
coef_third = 2.0315

Z, LAYERS, Y, CORES = 8, 2, 4, 2
UNITS = Y * CORES


def from_z(x, step):
    pairs = [
        (((z + step) % Z) * LAYERS + layer, z * LAYERS + layer)
        for z in range(Z)
        for layer in range(LAYERS)
    ]
    return lax.ppermute(x, "row", pairs)


def from_layer(x):
    return lax.ppermute(x, "row", [(i ^ 1, i) for i in range(Z * LAYERS)])


def from_core(x):
    return lax.ppermute(x, "col", [(i ^ 1, i) for i in range(Y * CORES)])


def from_y(x, step):
    pairs = [
        (((y + step) % Y) * CORES + core, y * CORES + core)
        for y in range(Y)
        for core in range(CORES)
    ]
    return lax.ppermute(x, "col", pairs)


def ring(block):
    half = block.shape[0] // 2
    parts = [block[:half], block[half:]]
    got = {0: list(parts)}
    up, down = list(parts), list(parts)
    for step in range(1, Z // 2):
        got[step], got[Z - step] = [None, None], [None, None]
        for h in range(2):
            up[h] = from_z(up[h], 1)
            got[step][h] = up[h]
            down[1 - h] = from_z(down[1 - h], -1)
            got[Z - step][1 - h] = down[1 - h]
    got[Z // 2] = [from_z(up[0], 1), from_z(down[1], -1)]
    return got


def nt(left, right):
    return lax.dot_general(
        left, right, (((1,), (1,)), ((), ())), preferred_element_type=jnp.float32
    )


def tn(left, right):
    return lax.dot_general(
        left, right, (((0,), (0,)), ((), ())), preferred_element_type=jnp.float32
    )


def per_device(iterate):
    rows, cols = iterate.shape
    unit = rows // UNITS
    width = cols * lax.axis_size("col")
    me = lax.axis_index("col")
    order = jnp.arange(UNITS)
    place = ((me // CORES + order // CORES) % Y) * CORES + (me % CORES + order % CORES) % CORES
    turned = iterate.reshape(UNITS, unit, cols)[place].reshape(rows, cols)

    other = from_layer(iterate)
    own_cols = jnp.concatenate([iterate, other], axis=0)
    panel = ring(turned)

    wide = own_cols.shape[0]

    def summed(steps):
        term = jnp.concatenate([nt(part, own_cols) for s in steps for part in panel[s]], axis=0)
        term = term.reshape(len(steps), Y, CORES, unit, wide)
        pair = term[:, :, 0] + from_core(term[:, :, 1].astype(jnp.bfloat16)).astype(jnp.float32)
        total = pair[:, 0]
        for j in range(1, Y):
            total = total + from_y(pair[:, j].astype(jnp.bfloat16), -j).astype(jnp.float32)
        return (total / width).astype(jnp.bfloat16)

    first, second = [0, 1, 7, 2, 6], [3, 5, 4]
    early, late = summed(first), summed(second)
    by_step = {s: early[i] for i, s in enumerate(first)} | {s: late[i] for i, s in enumerate(second)}
    gram = jnp.stack([by_step[s] for s in range(Z)])

    around = ring(gram.reshape(Z * unit, wide))
    across = []
    for s in range(Z):
        piece = jnp.concatenate(around[s], axis=0).reshape(Z, unit, wide)
        across.append(jnp.roll(piece, s, axis=0).reshape(Z * unit, wide))

    theirs = from_layer(jnp.concatenate([gram[..., rows:], gram[..., :rows]], axis=-1))

    def column(mine):
        got = jnp.stack([mine] + [from_y(mine, j) for j in range(1, Y)])
        both = jnp.stack([got, from_core(got)], axis=1)
        both = both.reshape(UNITS, Z, unit, wide)
        back = jnp.zeros((UNITS,), jnp.int32).at[place].set(order.astype(jnp.int32))
        return both[back].transpose(1, 0, 2, 3).reshape(Z, rows, wide)

    down = jnp.stack([column(gram), column(theirs)], axis=1).reshape(Z * wide, wide)
    square = jnp.dot(jnp.concatenate(across, axis=1), down, preferred_element_type=jnp.float32)
    mine = gram.reshape(Z * unit, wide).astype(jnp.float32)
    poly = (coef_second * mine + coef_third * square).astype(jnp.bfloat16).reshape(Z, unit, wide)

    got = jnp.stack([poly] + [from_y(poly, j) for j in range(1, Y)])
    both = jnp.stack([got, from_core(got)], axis=1)
    both = both.transpose(2, 0, 1, 3, 4).reshape(Z * rows, wide)
    whole = jnp.concatenate([part for s in range(Z) for part in panel[s]], axis=0)
    applied = tn(both, whole)
    add = from_layer(applied[rows:].astype(jnp.bfloat16)).astype(jnp.float32)
    return (coef_first * iterate.astype(jnp.float32) + applied[:rows] + add).astype(jnp.bfloat16)


def solution(mesh):
    return jax.shard_map(
        per_device,
        mesh=mesh,
        in_specs=(P(("wa", "row"), "col"),),
        out_specs=P(("wa", "row"), "col"),
        check_vma=False,
    )
```

```python
import functools

import jax
import jax.numpy as jnp
from jax import lax
from jax.experimental import pallas as pl
from jax.experimental.pallas import tpu as pltpu
from jax.sharding import PartitionSpec as P

coef_first = 3.4445
coef_second = -4.775
coef_third = 2.0315

Z, LAYERS, Y, CORES = 8, 2, 4, 2
UNITS = Y * CORES
EARLY, LATE = (0, 1, 7, 2, 6), (3, 5, 4)


def from_z(x, step):
    pairs = [
        (((z + step) % Z) * LAYERS + layer, z * LAYERS + layer)
        for z in range(Z)
        for layer in range(LAYERS)
    ]
    return lax.ppermute(x, "row", pairs)


def from_layer(x):
    return lax.ppermute(x, "row", [(i ^ 1, i) for i in range(Z * LAYERS)])


def from_core(x):
    return lax.ppermute(x, "col", [(i ^ 1, i) for i in range(Y * CORES)])


def from_y(x, step):
    pairs = [
        (((y + step) % Y) * CORES + core, y * CORES + core)
        for y in range(Y)
        for core in range(CORES)
    ]
    return lax.ppermute(x, "col", pairs)


def ring(block):
    half = block.shape[0] // 2
    got = {0: (block,)}
    up = down = block
    for step in range(1, Z // 2):
        up, down = from_z(up, 1), from_z(down, -1)
        got[step], got[Z - step] = (up,), (down,)
    got[Z // 2] = (from_z(up[:half], 1), from_z(down[half:], -1))
    return got


def nt(left, right):
    return lax.dot_general(
        left, right, (((1,), (1,)), ((), ())), preferred_element_type=jnp.float32
    )


def tn(left, right):
    return lax.dot_general(
        left, right, (((0,), (0,)), ((), ())), preferred_element_type=jnp.float32
    )


def local(body, out, scratch=(), flops=0):
    def call(*args):
        moved = sum(a.size * a.dtype.itemsize for a in args)
        return pl.pallas_call(
            body,
            out_shape=out,
            in_specs=[pl.BlockSpec(memory_space=pltpu.VMEM) for _ in args],
            out_specs=jax.tree.map(lambda _: pl.BlockSpec(memory_space=pltpu.VMEM), out),
            scratch_shapes=list(scratch),
            compiler_params=pltpu.CompilerParams(vmem_limit_bytes=28 * 2**20),
            cost_estimate=pl.CostEstimate(flops=flops, bytes_accessed=moved, transcendentals=0),
        )(*args)

    return call


def gram_body(counts, *refs):
    blocks, (own, other, keep, send) = refs[: sum(counts)], refs[sum(counts) :]
    rows = own.shape[0]
    unit = rows // UNITS
    at = 0
    for b, count in enumerate(counts):
        start = 0
        for _ in range(count):
            part = blocks[at][...]
            at += 1
            for layer, side in enumerate((own, other)):
                term = nt(part, side[...])
                cols = slice(layer * rows, (layer + 1) * rows)
                for i in range(part.shape[0] // unit):
                    u = start + i
                    piece = term[i * unit : (i + 1) * unit]
                    if u % CORES == 0:
                        keep[b, u // CORES, :, cols] = piece
                    else:
                        send[b, u // CORES, :, cols] = piece.astype(send.dtype)
            start += part.shape[0] // unit


def finish_body(order, width, *refs):
    groups = (len(refs) - 3) // 4
    turn, gram, flipped = refs[-3:]
    rows = turn.shape[0]
    unit = gram.shape[1]
    for g in range(groups):
        first, rest = refs[4 * g], refs[4 * g + 1 : 4 * g + 4]
        for i, s in enumerate(order[g]):
            total = first[i]
            for r in rest:
                total = total + r[i].astype(jnp.float32)
            gram[s] = (total / width).astype(gram.dtype)
    flat = gram[...].reshape(Z * unit, LAYERS * rows)
    for layer in range(LAYERS):
        cols = slice(layer * rows, (layer + 1) * rows)
        flipped[:, cols] = nt(flat[:, cols], turn[...]).astype(flipped.dtype)


def poly_body(*refs):
    around, refs = refs[: Z + 1], refs[Z + 1 :]
    mine, theirs, (gram, out, down) = refs[:UNITS], refs[UNITS : 2 * UNITS], refs[2 * UNITS :]
    unit, wide = gram.shape[1], gram.shape[2]
    rows = wide // LAYERS
    for s in range(Z):
        for u in range(UNITS):
            at = s * wide + u * unit
            down[at : at + unit, :] = mine[u][s]
            down[at + rows : at + rows + unit, :rows] = theirs[u][s, :, rows:]
            down[at + rows : at + rows + unit, rows:] = theirs[u][s, :, :rows]
    blocks = [around[s][...] for s in range(Z // 2)]
    blocks.append(jnp.concatenate([around[Z // 2][...], around[Z // 2 + 1][...]], axis=0))
    blocks += [around[s + 1][...] for s in range(Z // 2 + 1, Z)]
    total = coef_second * gram[...].reshape(Z * unit, wide).astype(jnp.float32)
    for s in range(Z):
        part = jnp.dot(blocks[s], down[s * wide : (s + 1) * wide, :], preferred_element_type=jnp.float32)
        if s:
            cut = (Z - s) * unit
            part = jnp.concatenate([part[cut:], part[:cut]], axis=0)
        total = total + coef_third * part
    out[...] = total.astype(out.dtype).reshape(Z, unit, wide)


def apply_body(counts, layer, scaled, *refs):
    pieces, refs = refs[:UNITS], refs[UNITS:]
    panel, refs = refs[: sum(counts)], refs[sum(counts) :]
    poly, out = refs[-1], refs[-2]
    unit, wide = pieces[0].shape[1], pieces[0].shape[2]
    rows = wide // LAYERS
    for s in range(Z):
        for u in range(UNITS):
            at = s * rows + u * unit
            poly[at : at + unit, :] = pieces[u][s, :, layer * rows : (layer + 1) * rows]
    total, at, start = None, 0, 0
    for r in range(sum(counts)):
        block = panel[r][...]
        term = tn(poly[start : start + block.shape[0], :], block)
        total = term if total is None else total + term
        start += block.shape[0]
    if scaled:
        total = coef_first * refs[0][...].astype(jnp.float32) + total
    out[...] = total.astype(out.dtype)


def chosen(rows, unit):
    me = lax.axis_index("col")
    to = lax.broadcasted_iota(jnp.int32, (rows, rows), 0)
    at = lax.broadcasted_iota(jnp.int32, (rows, rows), 1)
    u = to // unit
    source = (me // CORES + u // CORES) % Y * CORES + (me + u) % CORES
    return (at == source * unit + to % unit).astype(jnp.bfloat16)


def per_device(iterate):
    rows, cols = iterate.shape
    unit = rows // UNITS
    width = cols * lax.axis_size("col")
    wide = LAYERS * rows
    half = jnp.bfloat16
    turn = chosen(rows, unit)
    turned = jnp.dot(turn, iterate, preferred_element_type=jnp.float32).astype(half)

    other = from_layer(iterate)
    panel = ring(turned)

    def sums(steps):
        n = len(steps)
        parts = [part for s in steps for part in panel[s]]
        keep, send = local(
            functools.partial(gram_body, [len(panel[s]) for s in steps]),
            (
                jax.ShapeDtypeStruct((n, Y, unit, wide), jnp.float32),
                jax.ShapeDtypeStruct((n, Y, unit, wide), half),
            ),
            flops=2 * n * rows * wide * cols,
        )(*parts, iterate, other)
        pair = keep + from_core(send).astype(jnp.float32)
        return [pair[:, 0]] + [from_y(pair[:, j].astype(half), -j) for j in range(1, Y)]

    gram, flipped = local(
        functools.partial(finish_body, (EARLY, LATE), width),
        (
            jax.ShapeDtypeStruct((Z, unit, wide), half),
            jax.ShapeDtypeStruct((Z * unit, wide), half),
        ),
    )(*sums(EARLY), *sums(LATE), turn)

    def column(mine):
        got = [mine] + [from_y(mine, j) for j in range(1, Y)]
        return [piece for g in got for piece in (g, from_core(g))]

    theirs = from_layer(gram)
    around = ring(flipped)
    poly = local(
        poly_body,
        jax.ShapeDtypeStruct((Z, unit, wide), half),
        [pltpu.VMEM((Z * wide, wide), half)],
        flops=2 * rows * wide * Z * wide,
    )(*[part for s in range(Z) for part in around[s]], *column(gram), *column(theirs), gram)

    pieces = column(poly)
    parts = [part for s in range(Z) for part in panel[s]]
    counts = [len(panel[s]) for s in range(Z)]

    def product(layer, scaled, *more):
        return local(
            functools.partial(apply_body, counts, layer, scaled),
            jax.ShapeDtypeStruct((rows, cols), jnp.float32 if scaled else half),
            [pltpu.VMEM((Z * rows, rows), half)],
            flops=2 * rows * Z * rows * cols,
        )(*pieces, *parts, *more)

    add = from_layer(product(1, False))
    mine = product(0, True, iterate)
    return (mine + add.astype(jnp.float32)).astype(half)


def solution(mesh):
    return jax.shard_map(
        per_device,
        mesh=mesh,
        in_specs=(P(("wa", "row"), "col"),),
        out_specs=P(("wa", "row"), "col"),
        check_vma=False,
    )
```

```python
import functools

import jax
import jax.numpy as jnp
from jax import lax
from jax.experimental import pallas as pl
from jax.experimental.pallas import tpu as pltpu
from jax.sharding import PartitionSpec as P

coef_first = 3.4445
coef_second = -4.775
coef_third = 2.0315

Z, LAYERS, Y, CORES = 8, 2, 4, 2
UNITS = Y * CORES
GROUPS = ((0, 1, 7, 2, 6), (3, 5, 4))


def from_z(x, step):
    pairs = [
        (((z + step) % Z) * LAYERS + layer, z * LAYERS + layer)
        for z in range(Z)
        for layer in range(LAYERS)
    ]
    return lax.ppermute(x, "row", pairs)


def from_layer(x):
    return lax.ppermute(x, "row", [(i ^ 1, i) for i in range(Z * LAYERS)])


def from_core(x):
    return lax.ppermute(x, "col", [(i ^ 1, i) for i in range(Y * CORES)])


def from_y(x, step):
    pairs = [
        (((y + step) % Y) * CORES + core, y * CORES + core)
        for y in range(Y)
        for core in range(CORES)
    ]
    return lax.ppermute(x, "col", pairs)


def ring(block, chunks=2):
    size = block.shape[0] // chunks
    up = [block[i * size : (i + 1) * size] for i in range(chunks)]
    down = list(up)
    got = {0: (block,)}
    for step in range(1, Z // 2):
        for i in range(chunks):
            up[i], down[i] = from_z(up[i], 1), from_z(down[i], -1)
        got[step], got[Z - step] = tuple(up), tuple(down)
    half = block.shape[0] // 2
    if chunks == 1:
        got[Z // 2] = (from_z(up[0][:half], 1), from_z(down[0][half:], -1))
    else:
        lower = tuple(from_z(p, 1) for p in up[: chunks // 2])
        got[Z // 2] = lower + tuple(from_z(p, -1) for p in down[chunks // 2 :])
    return got


def nt(left, right):
    return lax.dot_general(
        left, right, (((1,), (1,)), ((), ())), preferred_element_type=jnp.float32
    )


def tn(left, right):
    return lax.dot_general(
        left, right, (((0,), (0,)), ((), ())), preferred_element_type=jnp.float32
    )


def local(body, out, scratch=(), flops=0):
    def call(*args):
        moved = sum(a.size * a.dtype.itemsize for a in args)
        return pl.pallas_call(
            body,
            out_shape=out,
            in_specs=[pl.BlockSpec(memory_space=pltpu.SMEM)]
            + [pl.BlockSpec(memory_space=pltpu.VMEM) for _ in args[1:]],
            out_specs=jax.tree.map(lambda _: pl.BlockSpec(memory_space=pltpu.VMEM), out),
            scratch_shapes=list(scratch),
            compiler_params=pltpu.CompilerParams(vmem_limit_bytes=28 * 2**20),
            cost_estimate=pl.CostEstimate(flops=flops, bytes_accessed=moved, transcendentals=0),
        )(*args)

    return call


def place(me, i):
    j, e = i // CORES, i % CORES
    y, core = me // CORES, me % CORES
    core = 1 - core if e else core
    return (y + j) % Y * CORES + core


def gram_body(counts, me, *refs):
    blocks, (own, other, keep, send, stack, term) = refs[: sum(counts)], refs[sum(counts) :]
    rows = own.shape[0]
    unit = rows // UNITS
    start = 0
    for ref in blocks:
        stack[start : start + ref.shape[0], :] = ref[...]
        start += ref.shape[0]
    for layer, side in enumerate((own, other)):
        cols = slice(layer * rows, (layer + 1) * rows)
        term[...] = nt(stack[...], side[...])
        for b in range(len(counts)):
            for u in range(UNITS):
                piece = term[pl.ds(b * rows + place(me[0], u) * unit, unit), :]
                if u % CORES == 0:
                    keep[b, u // CORES, :, cols] = piece
                else:
                    send[b, u // CORES, :, cols] = piece.astype(send.dtype)


def pair_body(groups, me, *refs):
    ins, (first, *rest) = refs[: 2 * len(groups)], refs[2 * len(groups) :]
    for g, steps in enumerate(groups):
        keep, got = ins[2 * g], ins[2 * g + 1]
        for i, s in enumerate(steps):
            first[s] = keep[i, 0] + got[i, 0].astype(jnp.float32)
            for j in range(1, Y):
                rest[j - 1][s] = (keep[i, j] + got[i, j].astype(jnp.float32)).astype(rest[j - 1].dtype)


def finish_body(width, me, first, *refs):
    rest, gram = refs[:-1], refs[-1]
    total = first[...]
    for r in rest:
        total = total + r[...].astype(jnp.float32)
    gram[...] = (total / width).astype(gram.dtype)


def poly_body(counts, me, *refs):
    around, refs = refs[: sum(counts)], refs[sum(counts) :]
    mine, theirs, (gram, out, down) = refs[:UNITS], refs[UNITS : 2 * UNITS], refs[2 * UNITS :]
    unit, wide = gram.shape[1], gram.shape[2]
    rows = wide // LAYERS
    for s in range(Z):
        for u in range(UNITS):
            at = s * wide + place(me[0], u) * unit
            down[pl.ds(at, unit), :] = mine[u][s]
            down[pl.ds(at + rows, unit), :rows] = theirs[u][s, :, rows:]
            down[pl.ds(at + rows, unit), rows:] = theirs[u][s, :, :rows]
    total = coef_second * gram[...].reshape(Z * unit, wide).astype(jnp.float32)
    for s in range(Z):
        parts = [r[...] for r in around[sum(counts[:s]) : sum(counts[: s + 1])]]
        block = parts[0] if len(parts) == 1 else jnp.concatenate(parts, axis=0)
        part = jnp.dot(block, down[s * wide : (s + 1) * wide, :], preferred_element_type=jnp.float32)
        if s:
            cut = (Z - s) * unit
            part = jnp.concatenate([part[cut:], part[:cut]], axis=0)
        total = total + coef_third * part
    out[...] = total.astype(out.dtype).reshape(Z, unit, wide)


def apply_body(counts, layer, scaled, me, *refs):
    pieces, refs = refs[:UNITS], refs[UNITS:]
    panel, refs = refs[: sum(counts)], refs[sum(counts) :]
    poly, out = refs[-1], refs[-2]
    unit, wide = pieces[0].shape[1], pieces[0].shape[2]
    rows = wide // LAYERS
    for s in range(Z):
        for u in range(UNITS):
            at = s * rows + place(me[0], u) * unit
            poly[pl.ds(at, unit), :] = pieces[u][s, :, layer * rows : (layer + 1) * rows]
    total = None
    for s in range(Z):
        parts = [r[...] for r in panel[sum(counts[:s]) : sum(counts[: s + 1])]]
        block = parts[0] if len(parts) == 1 else jnp.concatenate(parts, axis=0)
        term = tn(poly[s * rows : (s + 1) * rows, :], block)
        total = term if total is None else total + term
    if scaled:
        total = coef_first * refs[0][...].astype(jnp.float32) + total
    out[...] = total.astype(out.dtype)


def per_device(iterate):
    rows, cols = iterate.shape
    unit = rows // UNITS
    width = cols * lax.axis_size("col")
    wide = LAYERS * rows
    half = jnp.bfloat16
    me = lax.axis_index("col").astype(jnp.int32).reshape(1)

    other = from_layer(iterate)
    panel = ring(iterate)

    def sums(steps):
        n = len(steps)
        parts = [part for s in steps for part in panel[s]]
        keep, send = local(
            functools.partial(gram_body, [len(panel[s]) for s in steps]),
            (
                jax.ShapeDtypeStruct((n, Y, unit, wide), jnp.float32),
                jax.ShapeDtypeStruct((n, Y, unit, wide), half),
            ),
            [pltpu.VMEM((n * rows, cols), half), pltpu.VMEM((n * rows, rows), jnp.float32)],
            flops=2 * n * rows * wide * cols,
        )(me, *parts, iterate, other)
        return keep, from_core(send)

    first, *rest = local(
        functools.partial(pair_body, GROUPS),
        [jax.ShapeDtypeStruct((Z, unit, wide), jnp.float32)]
        + [jax.ShapeDtypeStruct((Z, unit, wide), half)] * (Y - 1),
    )(me, *[t for g in GROUPS for t in sums(g)])
    gram = local(
        functools.partial(finish_body, width),
        jax.ShapeDtypeStruct((Z, unit, wide), half),
    )(me, first, *[from_y(r, -j) for j, r in enumerate(rest, 1)])

    def column(mine):
        got = [mine] + [from_y(mine, j) for j in range(1, Y)]
        return [piece for g in got for piece in (g, from_core(g))]

    bar = lax.optimization_barrier
    flat = gram.reshape(Z * unit, wide)
    theirs = from_layer(gram)
    mine = [gram] + [from_y(gram, j) for j in range(1, Y)]
    around = {0: (flat,)}
    up, down = from_z(flat, 1), from_z(flat, -1)
    around[1], around[7] = (up,), (down,)
    up, down, theirs = bar((up, down, theirs))
    more = [theirs] + [from_y(theirs, j) for j in range(1, Y)]
    up, down = from_z(up, 1), from_z(down, -1)
    around[2], around[6] = (up,), (down,)
    up, down, *mine = bar((up, down, *mine))
    mine = [piece for g in mine for piece in (g, from_core(g))]
    up, down = from_z(up, 1), from_z(down, -1)
    around[3], around[5] = (up,), (down,)
    up, down, *more = bar((up, down, *more))
    more = [piece for g in more for piece in (g, from_core(g))]
    size = Z * unit // 2
    around[4] = (from_z(up[:size], 1), from_z(down[size:], -1))
    poly = local(
        functools.partial(poly_body, [len(around[s]) for s in range(Z)]),
        jax.ShapeDtypeStruct((Z, unit, wide), half),
        [pltpu.VMEM((Z * wide, wide), half)],
        flops=2 * rows * wide * Z * wide,
    )(me, *[part for s in range(Z) for part in around[s]], *mine, *more, gram)

    pieces = column(poly)
    parts = [part for s in range(Z) for part in panel[s]]
    counts = [len(panel[s]) for s in range(Z)]

    def product(layer, scaled, *more):
        return local(
            functools.partial(apply_body, counts, layer, scaled),
            jax.ShapeDtypeStruct((rows, cols), jnp.float32 if scaled else half),
            [pltpu.VMEM((Z * rows, rows), half)],
            flops=2 * rows * Z * rows * cols,
        )(me, *pieces, *parts, *more)

    add = from_layer(product(1, False))
    mine = product(0, True, iterate)
    return (mine + add.astype(jnp.float32)).astype(half)


def solution(mesh):
    return jax.shard_map(
        per_device,
        mesh=mesh,
        in_specs=(P(("wa", "row"), "col"),),
        out_specs=P(("wa", "row"), "col"),
        check_vma=False,
    )
```

```python
import functools

import jax
import jax.numpy as jnp
from jax import lax
from jax.experimental import pallas as pl
from jax.experimental.pallas import tpu as pltpu
from jax.sharding import PartitionSpec as P

coef_first = 3.4445
coef_second = -4.775
coef_third = 2.0315

Z, LAYERS, Y, CORES = 8, 2, 4, 2
UNITS = Y * CORES
GROUPS = ((0, 1, 7, 2, 6), (3, 5, 4))


def from_z(x, step):
    pairs = [
        (((z + step) % Z) * LAYERS + layer, z * LAYERS + layer)
        for z in range(Z)
        for layer in range(LAYERS)
    ]
    return lax.ppermute(x, "row", pairs)


def from_layer(x):
    return lax.ppermute(x, "row", [(i ^ 1, i) for i in range(Z * LAYERS)])


def from_core(x):
    return lax.ppermute(x, "col", [(i ^ 1, i) for i in range(Y * CORES)])


def from_y(x, step):
    pairs = [
        (((y + step) % Y) * CORES + core, y * CORES + core)
        for y in range(Y)
        for core in range(CORES)
    ]
    return lax.ppermute(x, "col", pairs)


def ring(block, chunks=2):
    size = block.shape[0] // chunks
    up = [block[i * size : (i + 1) * size] for i in range(chunks)]
    down = list(up)
    got = {0: (block,)}
    for step in range(1, Z // 2):
        for i in range(chunks):
            up[i], down[i] = from_z(up[i], 1), from_z(down[i], -1)
        got[step], got[Z - step] = tuple(up), tuple(down)
    half = block.shape[0] // 2
    if chunks == 1:
        got[Z // 2] = (from_z(up[0][:half], 1), from_z(down[0][half:], -1))
    else:
        lower = tuple(from_z(p, 1) for p in up[: chunks // 2])
        got[Z // 2] = lower + tuple(from_z(p, -1) for p in down[chunks // 2 :])
    return got


def nt(left, right):
    return lax.dot_general(
        left, right, (((1,), (1,)), ((), ())), preferred_element_type=jnp.float32
    )


def tn(left, right):
    return lax.dot_general(
        left, right, (((0,), (0,)), ((), ())), preferred_element_type=jnp.float32
    )


def local(body, out, scratch=(), flops=0):
    def call(*args):
        moved = sum(a.size * a.dtype.itemsize for a in args)
        return pl.pallas_call(
            body,
            out_shape=out,
            in_specs=[pl.BlockSpec(memory_space=pltpu.SMEM)]
            + [pl.BlockSpec(memory_space=pltpu.VMEM) for _ in args[1:]],
            out_specs=jax.tree.map(lambda _: pl.BlockSpec(memory_space=pltpu.VMEM), out),
            scratch_shapes=list(scratch),
            compiler_params=pltpu.CompilerParams(vmem_limit_bytes=28 * 2**20),
            cost_estimate=pl.CostEstimate(flops=flops, bytes_accessed=moved, transcendentals=0),
        )(*args)

    return call


def place(me, i):
    j, e = i // CORES, i % CORES
    y, core = me // CORES, me % CORES
    core = 1 - core if e else core
    return (y + j) % Y * CORES + core


def gram_body(counts, me, *refs):
    blocks, (own, other, keep, send, stack, term) = refs[: sum(counts)], refs[sum(counts) :]
    rows = own.shape[0]
    unit = rows // UNITS
    start = 0
    for ref in blocks:
        stack[start : start + ref.shape[0], :] = ref[...]
        start += ref.shape[0]
    for layer, side in enumerate((own, other)):
        cols = slice(layer * rows, (layer + 1) * rows)
        term[...] = nt(stack[...], side[...])
        for b in range(len(counts)):
            for u in range(UNITS):
                piece = term[pl.ds(b * rows + place(me[0], u) * unit, unit), :]
                if u % CORES == 0:
                    keep[b, u // CORES, :, cols] = piece
                else:
                    send[b, u // CORES, :, cols] = piece.astype(send.dtype)


def pair_body(groups, me, *refs):
    ins, (first, *rest) = refs[: 2 * len(groups)], refs[2 * len(groups) :]
    for g, steps in enumerate(groups):
        keep, got = ins[2 * g], ins[2 * g + 1]
        for i, s in enumerate(steps):
            first[s] = keep[i, 0] + got[i, 0].astype(jnp.float32)
            for j in range(1, Y):
                rest[j - 1][s] = (keep[i, j] + got[i, j].astype(jnp.float32)).astype(rest[j - 1].dtype)


def finish_body(width, me, first, *refs):
    rest, gram = refs[:-1], refs[-1]
    total = first[...]
    for r in rest:
        total = total + r[...].astype(jnp.float32)
    gram[...] = (total / width).astype(gram.dtype)


def poly_body(counts, me, *refs):
    around, refs = refs[: sum(counts)], refs[sum(counts) :]
    mine, theirs, (gram, *outs, down) = refs[:UNITS], refs[UNITS : 2 * UNITS], refs[2 * UNITS :]
    unit, wide = gram.shape[1], gram.shape[2]
    rows = wide // LAYERS
    for s in range(Z):
        for u in range(UNITS):
            at = s * wide + place(me[0], u) * unit
            down[pl.ds(at, unit), :] = mine[u][s]
            down[pl.ds(at + rows, unit), :rows] = theirs[u][s, :, rows:]
            down[pl.ds(at + rows, unit), rows:] = theirs[u][s, :, :rows]
    total = coef_second * gram[...].reshape(Z * unit, wide).astype(jnp.float32)
    for s in range(Z):
        parts = [r[...] for r in around[sum(counts[:s]) : sum(counts[: s + 1])]]
        block = parts[0] if len(parts) == 1 else jnp.concatenate(parts, axis=0)
        part = jnp.dot(block, down[s * wide : (s + 1) * wide, :], preferred_element_type=jnp.float32)
        if s:
            cut = (Z - s) * unit
            part = jnp.concatenate([part[cut:], part[:cut]], axis=0)
        total = total + coef_third * part
    for layer, out in enumerate(outs):
        half = total[:, layer * rows : (layer + 1) * rows]
        out[...] = half.astype(out.dtype).reshape(Z, unit, rows)


def apply_body(counts, scaled, me, *refs):
    pieces, refs = refs[:UNITS], refs[UNITS:]
    panel, refs = refs[: sum(counts)], refs[sum(counts) :]
    poly, out = refs[-1], refs[-2]
    unit, rows = pieces[0].shape[1], pieces[0].shape[2]
    for s in range(Z):
        for u in range(UNITS):
            poly[pl.ds(s * rows + place(me[0], u) * unit, unit), :] = pieces[u][s]
    total = None
    for s in range(Z):
        parts = [r[...] for r in panel[sum(counts[:s]) : sum(counts[: s + 1])]]
        block = parts[0] if len(parts) == 1 else jnp.concatenate(parts, axis=0)
        term = tn(poly[s * rows : (s + 1) * rows, :], block)
        total = term if total is None else total + term
    if scaled:
        total = coef_first * refs[0][...].astype(jnp.float32) + total
    out[...] = total.astype(out.dtype)


def per_device(iterate):
    rows, cols = iterate.shape
    unit = rows // UNITS
    width = cols * lax.axis_size("col")
    wide = LAYERS * rows
    half = jnp.bfloat16
    me = lax.axis_index("col").astype(jnp.int32).reshape(1)

    other = from_layer(iterate)
    panel = ring(iterate)

    def sums(steps):
        n = len(steps)
        parts = [part for s in steps for part in panel[s]]
        keep, send = local(
            functools.partial(gram_body, [len(panel[s]) for s in steps]),
            (
                jax.ShapeDtypeStruct((n, Y, unit, wide), jnp.float32),
                jax.ShapeDtypeStruct((n, Y, unit, wide), half),
            ),
            [pltpu.VMEM((n * rows, cols), half), pltpu.VMEM((n * rows, rows), jnp.float32)],
            flops=2 * n * rows * wide * cols,
        )(me, *parts, iterate, other)
        return keep, from_core(send)

    first, *rest = local(
        functools.partial(pair_body, GROUPS),
        [jax.ShapeDtypeStruct((Z, unit, wide), jnp.float32)]
        + [jax.ShapeDtypeStruct((Z, unit, wide), half)] * (Y - 1),
    )(me, *[t for g in GROUPS for t in sums(g)])
    gram = local(
        functools.partial(finish_body, width),
        jax.ShapeDtypeStruct((Z, unit, wide), half),
    )(me, first, *[from_y(r, -j) for j, r in enumerate(rest, 1)])

    def column(mine):
        got = [mine] + [from_y(mine, j) for j in range(1, Y)]
        return [piece for g in got for piece in (g, from_core(g))]

    bar = lax.optimization_barrier
    flat = gram.reshape(Z * unit, wide)
    theirs = from_layer(gram)
    mine = [gram] + [from_y(gram, j) for j in range(1, Y)]
    around = {0: (flat,)}
    up, down = from_z(flat, 1), from_z(flat, -1)
    around[1], around[7] = (up,), (down,)
    up, down, theirs = bar((up, down, theirs))
    more = [theirs] + [from_y(theirs, j) for j in range(1, Y)]
    up, down = from_z(up, 1), from_z(down, -1)
    around[2], around[6] = (up,), (down,)
    up, down, *mine = bar((up, down, *mine))
    mine = [piece for g in mine for piece in (g, from_core(g))]
    up, down = from_z(up, 1), from_z(down, -1)
    around[3], around[5] = (up,), (down,)
    up, down, *more = bar((up, down, *more))
    more = [piece for g in more for piece in (g, from_core(g))]
    around[4] = (from_z(up, 1),)
    poly = local(
        functools.partial(poly_body, [len(around[s]) for s in range(Z)]),
        [jax.ShapeDtypeStruct((Z, unit, rows), half)] * LAYERS,
        [pltpu.VMEM((Z * wide, wide), half)],
        flops=2 * rows * wide * Z * wide,
    )(me, *[part for s in range(Z) for part in around[s]], *mine, *more, gram)

    def column(mine):
        got = [mine] + [from_y(mine, j) for j in range(1, Y)]
        return [piece for g in got for piece in (g, from_core(g))]

    parts = [part for s in range(Z) for part in panel[s]]
    counts = [len(panel[s]) for s in range(Z)]

    def product(pieces, scaled, *more):
        return local(
            functools.partial(apply_body, counts, scaled),
            jax.ShapeDtypeStruct((rows, cols), jnp.float32 if scaled else half),
            [pltpu.VMEM((Z * rows, rows), half)],
            flops=2 * rows * Z * rows * cols,
        )(me, *pieces, *parts, *more)

    add = product(column(poly[1]), False)
    own = poly[0]
    add = from_layer(add)
    mine = product(column(own), True, iterate)
    return (mine + add.astype(jnp.float32)).astype(half)


def solution(mesh):
    return jax.shard_map(
        per_device,
        mesh=mesh,
        in_specs=(P(("wa", "row"), "col"),),
        out_specs=P(("wa", "row"), "col"),
        check_vma=False,
    )
```

```python
import functools

import jax
import jax.numpy as jnp
from jax import lax
from jax.experimental import pallas as pl
from jax.experimental.pallas import tpu as pltpu
from jax.sharding import PartitionSpec as P

coef_first = 3.4445
coef_second = -4.775
coef_third = 2.0315

Z, LAYERS, Y, CORES = 8, 2, 4, 2
UNITS = Y * CORES
GROUPS = ((0, 1, 7, 2, 6, 3, 5), (4,))


def from_z(x, step):
    pairs = [
        (((z + step) % Z) * LAYERS + layer, z * LAYERS + layer)
        for z in range(Z)
        for layer in range(LAYERS)
    ]
    return lax.ppermute(x, "row", pairs)


def from_layer(x):
    return lax.ppermute(x, "row", [(i ^ 1, i) for i in range(Z * LAYERS)])


def from_core(x):
    return lax.ppermute(x, "col", [(i ^ 1, i) for i in range(Y * CORES)])


def from_y(x, step):
    pairs = [
        (((y + step) % Y) * CORES + core, y * CORES + core)
        for y in range(Y)
        for core in range(CORES)
    ]
    return lax.ppermute(x, "col", pairs)


def ring(block, chunks=2):
    size = block.shape[0] // chunks
    up = [block[i * size : (i + 1) * size] for i in range(chunks)]
    down = list(up)
    got = {0: (block,)}
    for step in range(1, Z // 2):
        for i in range(chunks):
            up[i], down[i] = from_z(up[i], 1), from_z(down[i], -1)
        got[step], got[Z - step] = tuple(up), tuple(down)
    half = block.shape[0] // 2
    if chunks == 1:
        got[Z // 2] = (from_z(up[0][:half], 1), from_z(down[0][half:], -1))
    else:
        lower = tuple(from_z(p, 1) for p in up[: chunks // 2])
        got[Z // 2] = lower + tuple(from_z(p, -1) for p in down[chunks // 2 :])
    return got


def nt(left, right):
    return lax.dot_general(
        left, right, (((1,), (1,)), ((), ())), preferred_element_type=jnp.float32
    )


def tn(left, right):
    return lax.dot_general(
        left, right, (((0,), (0,)), ((), ())), preferred_element_type=jnp.float32
    )


def local(body, out, scratch=(), flops=0):
    def call(*args):
        moved = sum(a.size * a.dtype.itemsize for a in args)
        return pl.pallas_call(
            body,
            out_shape=out,
            in_specs=[pl.BlockSpec(memory_space=pltpu.SMEM)]
            + [pl.BlockSpec(memory_space=pltpu.VMEM) for _ in args[1:]],
            out_specs=jax.tree.map(lambda _: pl.BlockSpec(memory_space=pltpu.VMEM), out),
            scratch_shapes=list(scratch),
            compiler_params=pltpu.CompilerParams(vmem_limit_bytes=28 * 2**20),
            cost_estimate=pl.CostEstimate(flops=flops, bytes_accessed=moved, transcendentals=0),
        )(*args)

    return call


def place(me, i):
    j, e = i // CORES, i % CORES
    y, core = me // CORES, me % CORES
    core = 1 - core if e else core
    return (y + j) % Y * CORES + core


def gram_body(counts, me, *refs):
    blocks, (own, other, keep, send, stack, term) = refs[: sum(counts)], refs[sum(counts) :]
    rows = own.shape[0]
    unit = rows // UNITS
    start = 0
    for ref in blocks:
        stack[start : start + ref.shape[0], :] = ref[...]
        start += ref.shape[0]
    for layer, side in enumerate((own, other)):
        cols = slice(layer * rows, (layer + 1) * rows)
        term[...] = nt(stack[...], side[...])
        for b in range(len(counts)):
            for u in range(UNITS):
                piece = term[pl.ds(b * rows + place(me[0], u) * unit, unit), :]
                if u % CORES == 0:
                    keep[b, u // CORES, :, cols] = piece
                else:
                    send[b, u // CORES, :, cols] = piece.astype(send.dtype)


def pair_body(groups, me, *refs):
    ins, (first, *rest) = refs[: 2 * len(groups)], refs[2 * len(groups) :]
    for g, steps in enumerate(groups):
        keep, got = ins[2 * g], ins[2 * g + 1]
        for i, s in enumerate(steps):
            first[s] = keep[i, 0] + got[i, 0].astype(jnp.float32)
            for j in range(1, Y):
                rest[j - 1][s] = (keep[i, j] + got[i, j].astype(jnp.float32)).astype(rest[j - 1].dtype)


def finish_body(width, me, first, *refs):
    rest, gram = refs[:-1], refs[-1]
    total = first[...]
    for r in rest:
        total = total + r[...].astype(jnp.float32)
    gram[...] = (total / width).astype(gram.dtype)


def poly_body(counts, me, *refs):
    around, refs = refs[: sum(counts)], refs[sum(counts) :]
    mine, theirs, (gram, *outs, down) = refs[:UNITS], refs[UNITS : 2 * UNITS], refs[2 * UNITS :]
    unit, wide = gram.shape[1], gram.shape[2]
    rows = wide // LAYERS
    for s in range(Z):
        for u in range(UNITS):
            at = s * wide + place(me[0], u) * unit
            down[pl.ds(at, unit), :] = mine[u][s]
            down[pl.ds(at + rows, unit), :rows] = theirs[u][s, :, rows:]
            down[pl.ds(at + rows, unit), rows:] = theirs[u][s, :, :rows]
    total = coef_second * gram[...].reshape(Z * unit, wide).astype(jnp.float32)
    for s in range(Z):
        parts = [r[...] for r in around[sum(counts[:s]) : sum(counts[: s + 1])]]
        block = parts[0] if len(parts) == 1 else jnp.concatenate(parts, axis=0)
        part = jnp.dot(block, down[s * wide : (s + 1) * wide, :], preferred_element_type=jnp.float32)
        if s:
            cut = (Z - s) * unit
            part = jnp.concatenate([part[cut:], part[:cut]], axis=0)
        total = total + coef_third * part
    for layer, out in enumerate(outs):
        half = total[:, layer * rows : (layer + 1) * rows]
        out[...] = half.astype(out.dtype).reshape(Z, unit, rows)


def apply_body(counts, scaled, me, *refs):
    pieces, refs = refs[:UNITS], refs[UNITS:]
    panel, refs = refs[: sum(counts)], refs[sum(counts) :]
    poly, out = refs[-1], refs[-2]
    unit, rows = pieces[0].shape[1], pieces[0].shape[2]
    for s in range(Z):
        for u in range(UNITS):
            poly[pl.ds(s * rows + place(me[0], u) * unit, unit), :] = pieces[u][s]
    total = None
    for s in range(Z):
        parts = [r[...] for r in panel[sum(counts[:s]) : sum(counts[: s + 1])]]
        block = parts[0] if len(parts) == 1 else jnp.concatenate(parts, axis=0)
        term = tn(poly[s * rows : (s + 1) * rows, :], block)
        total = term if total is None else total + term
    if scaled:
        total = coef_first * refs[0][...].astype(jnp.float32) + total
    out[...] = total.astype(out.dtype)


def per_device(iterate):
    rows, cols = iterate.shape
    unit = rows // UNITS
    width = cols * lax.axis_size("col")
    wide = LAYERS * rows
    half = jnp.bfloat16
    me = lax.axis_index("col").astype(jnp.int32).reshape(1)

    other = from_layer(iterate)
    panel = ring(iterate)

    def sums(steps):
        n = len(steps)
        parts = [part for s in steps for part in panel[s]]
        keep, send = local(
            functools.partial(gram_body, [len(panel[s]) for s in steps]),
            (
                jax.ShapeDtypeStruct((n, Y, unit, wide), jnp.float32),
                jax.ShapeDtypeStruct((n, Y, unit, wide), half),
            ),
            [pltpu.VMEM((n * rows, cols), half), pltpu.VMEM((n * rows, rows), jnp.float32)],
            flops=2 * n * rows * wide * cols,
        )(me, *parts, iterate, other)
        return keep, send

    keep, send = sums(GROUPS[0])
    send, *last = lax.optimization_barrier((send, *panel[Z // 2]))
    panel[Z // 2] = tuple(last)
    late, late_send = sums(GROUPS[1])
    first, *rest = local(
        functools.partial(pair_body, GROUPS),
        [jax.ShapeDtypeStruct((Z, unit, wide), jnp.float32)]
        + [jax.ShapeDtypeStruct((Z, unit, wide), half)] * (Y - 1),
    )(me, keep, from_core(send), late, from_core(late_send))
    gram = local(
        functools.partial(finish_body, width),
        jax.ShapeDtypeStruct((Z, unit, wide), half),
    )(me, first, *[from_y(r, -j) for j, r in sorted(enumerate(rest, 1), key=lambda t: t[0] != 2)])

    def column(mine):
        got = [mine] + [from_y(mine, j) for j in range(1, Y)]
        return [piece for g in got for piece in (g, from_core(g))]

    bar = lax.optimization_barrier
    flat = gram.reshape(Z * unit, wide)
    theirs = from_layer(gram)
    mine = [gram] + [from_y(gram, j) for j in range(1, Y)]
    around = {0: (flat,)}
    up, down = from_z(flat, 1), from_z(flat, -1)
    around[1], around[7] = (up,), (down,)
    up, down, theirs = bar((up, down, theirs))
    more = [theirs, from_y(theirs, 1), None, from_y(theirs, 3)]
    up, down = from_z(up, 1), from_z(down, -1)
    around[2], around[6] = (up,), (down,)
    up, down, *mine = bar((up, down, *mine))
    more[2] = from_layer(mine[2])
    mine = [piece for g in mine for piece in (g, from_core(g))]
    up, down = from_z(up, 1), from_z(down, -1)
    around[3], around[5] = (up,), (down,)
    up, down, *more = bar((up, down, *more))
    more = [piece for g in more for piece in (g, from_core(g))]
    around[4] = (from_z(up, 1),)
    poly = local(
        functools.partial(poly_body, [len(around[s]) for s in range(Z)]),
        [jax.ShapeDtypeStruct((Z, unit, rows), half)] * LAYERS,
        [pltpu.VMEM((Z * wide, wide), half)],
        flops=2 * rows * wide * Z * wide,
    )(me, *[part for s in range(Z) for part in around[s]], *mine, *more, gram)

    def column(mine):
        far = from_y(mine, 2)
        got = [mine, from_y(mine, 1), far, from_y(mine, 3)]
        return [piece for g in got for piece in (g, from_core(g))]

    parts = [part for s in range(Z) for part in panel[s]]
    counts = [len(panel[s]) for s in range(Z)]

    def product(pieces, scaled, *more):
        return local(
            functools.partial(apply_body, counts, scaled),
            jax.ShapeDtypeStruct((rows, cols), jnp.float32 if scaled else half),
            [pltpu.VMEM((Z * rows, rows), half)],
            flops=2 * rows * Z * rows * cols,
        )(me, *pieces, *parts, *more)

    add = product(column(poly[1]), False)
    own = poly[0]
    add = from_layer(add)
    mine = product(column(own), True, iterate)
    return (mine + add.astype(jnp.float32)).astype(half)


def solution(mesh):
    return jax.shard_map(
        per_device,
        mesh=mesh,
        in_specs=(P(("wa", "row"), "col"),),
        out_specs=P(("wa", "row"), "col"),
        check_vma=False,
    )
```

```python
import functools

import jax
import jax.numpy as jnp
from jax import lax
from jax.experimental import pallas as pl
from jax.experimental.pallas import tpu as pltpu
from jax.sharding import PartitionSpec as P

coef_first = 3.4445
coef_second = -4.775
coef_third = 2.0315

Z, LAYERS, Y, CORES = 8, 2, 4, 2
UNITS = Y * CORES
GROUPS = ((0, 1, 7, 2, 6, 3, 5), (4,))


def from_z(x, step):
    pairs = [
        (((z + step) % Z) * LAYERS + layer, z * LAYERS + layer)
        for z in range(Z)
        for layer in range(LAYERS)
    ]
    return lax.ppermute(x, "row", pairs)


def from_layer(x):
    return lax.ppermute(x, "row", [(i ^ 1, i) for i in range(Z * LAYERS)])


def from_core(x):
    return lax.ppermute(x, "col", [(i ^ 1, i) for i in range(Y * CORES)])


def from_y(x, step):
    pairs = [
        (((y + step) % Y) * CORES + core, y * CORES + core)
        for y in range(Y)
        for core in range(CORES)
    ]
    return lax.ppermute(x, "col", pairs)


def ring(block, chunks=2):
    size = block.shape[0] // chunks
    up = [block[i * size : (i + 1) * size] for i in range(chunks)]
    down = list(up)
    got = {0: (block,)}
    for step in range(1, Z // 2):
        for i in range(chunks):
            up[i], down[i] = from_z(up[i], 1), from_z(down[i], -1)
        got[step], got[Z - step] = tuple(up), tuple(down)
    half = block.shape[0] // 2
    if chunks == 1:
        got[Z // 2] = (from_z(up[0][:half], 1), from_z(down[0][half:], -1))
    else:
        lower = tuple(from_z(p, 1) for p in up[: chunks // 2])
        got[Z // 2] = lower + tuple(from_z(p, -1) for p in down[chunks // 2 :])
    return got


def nt(left, right):
    return lax.dot_general(
        left, right, (((1,), (1,)), ((), ())), preferred_element_type=jnp.float32
    )


def tn(left, right):
    return lax.dot_general(
        left, right, (((0,), (0,)), ((), ())), preferred_element_type=jnp.float32
    )


def local(body, out, scratch=(), flops=0):
    def call(*args):
        moved = sum(a.size * a.dtype.itemsize for a in args)
        return pl.pallas_call(
            body,
            out_shape=out,
            in_specs=[pl.BlockSpec(memory_space=pltpu.SMEM)]
            + [pl.BlockSpec(memory_space=pltpu.VMEM) for _ in args[1:]],
            out_specs=jax.tree.map(lambda _: pl.BlockSpec(memory_space=pltpu.VMEM), out),
            scratch_shapes=list(scratch),
            compiler_params=pltpu.CompilerParams(vmem_limit_bytes=16 * 2**20),
            cost_estimate=pl.CostEstimate(flops=flops, bytes_accessed=moved, transcendentals=0),
        )(*args)

    return call


def place(me, i):
    j, e = i // CORES, i % CORES
    y, core = me // CORES, me % CORES
    core = 1 - core if e else core
    return (y + j) % Y * CORES + core


def turn_body(me, own, other, out):
    rows = own.shape[0]
    out[:, :rows] = own[...].T
    out[:, rows:] = other[...].T


def gram_body(counts, me, *refs):
    blocks, (turned, keep, send, stack, term) = refs[: sum(counts)], refs[sum(counts) :]
    rows = turned.shape[1] // LAYERS
    unit = rows // UNITS
    start = 0
    for ref in blocks:
        stack[start : start + ref.shape[0], :] = ref[...]
        start += ref.shape[0]
    for layer in range(LAYERS):
        cols = slice(layer * rows, (layer + 1) * rows)
        term[...] = jnp.dot(stack[...], turned[:, cols], preferred_element_type=jnp.float32)
        for b in range(len(counts)):
            for u in range(UNITS):
                piece = term[pl.ds(b * rows + place(me[0], u) * unit, unit), :]
                if u % CORES == 0:
                    keep[b, u // CORES, :, cols] = piece
                else:
                    send[b, u // CORES, :, cols] = piece.astype(send.dtype)


def pair_body(groups, me, *refs):
    ins, (first, *rest) = refs[: 2 * len(groups)], refs[2 * len(groups) :]
    for g, steps in enumerate(groups):
        keep, got = ins[2 * g], ins[2 * g + 1]
        for i, s in enumerate(steps):
            first[s] = keep[i, 0] + got[i, 0].astype(jnp.float32)
            for j in range(1, Y):
                rest[j - 1][s] = (keep[i, j] + got[i, j].astype(jnp.float32)).astype(rest[j - 1].dtype)


def finish_body(width, me, first, *refs):
    rest, gram = refs[:-1], refs[-1]
    total = first[...]
    for r in rest:
        total = total + r[...].astype(jnp.float32)
    gram[...] = (total / width).astype(gram.dtype)


def poly_body(counts, me, *refs):
    around, refs = refs[: sum(counts)], refs[sum(counts) :]
    mine, theirs, (gram, *outs, down) = refs[:UNITS], refs[UNITS : 2 * UNITS], refs[2 * UNITS :]
    unit, wide = gram.shape[1], gram.shape[2]
    rows = wide // LAYERS
    for s in range(Z):
        for u in range(UNITS):
            at = s * wide + place(me[0], u) * unit
            down[pl.ds(at, unit), :] = mine[u][s]
            down[pl.ds(at + rows, unit), :rows] = theirs[u][s, :, rows:]
            down[pl.ds(at + rows, unit), rows:] = theirs[u][s, :, :rows]
    total = coef_second * gram[...].reshape(Z * unit, wide).astype(jnp.float32)
    for s in range(Z):
        parts = [r[...] for r in around[sum(counts[:s]) : sum(counts[: s + 1])]]
        block = parts[0] if len(parts) == 1 else jnp.concatenate(parts, axis=0)
        part = jnp.dot(block, down[s * wide : (s + 1) * wide, :], preferred_element_type=jnp.float32)
        if s:
            cut = (Z - s) * unit
            part = jnp.concatenate([part[cut:], part[:cut]], axis=0)
        total = total + coef_third * part
    for layer, out in enumerate(outs):
        half = total[:, layer * rows : (layer + 1) * rows]
        out[...] = half.astype(out.dtype).reshape(Z, unit, rows)


def apply_body(counts, scaled, me, *refs):
    pieces, refs = refs[:UNITS], refs[UNITS:]
    panel, refs = refs[: sum(counts)], refs[sum(counts) :]
    poly, out = refs[-1], refs[-2]
    unit, rows = pieces[0].shape[1], pieces[0].shape[2]
    for s in range(Z):
        for u in range(UNITS):
            poly[pl.ds(s * rows + place(me[0], u) * unit, unit), :] = pieces[u][s]
    total = None
    for s in range(Z):
        parts = [r[...] for r in panel[sum(counts[:s]) : sum(counts[: s + 1])]]
        block = parts[0] if len(parts) == 1 else jnp.concatenate(parts, axis=0)
        term = tn(poly[s * rows : (s + 1) * rows, :], block)
        total = term if total is None else total + term
    if scaled:
        total = coef_first * refs[0][...].astype(jnp.float32) + total
    out[...] = total.astype(out.dtype)


def per_device(iterate):
    rows, cols = iterate.shape
    unit = rows // UNITS
    width = cols * lax.axis_size("col")
    wide = LAYERS * rows
    half = jnp.bfloat16
    me = lax.axis_index("col").astype(jnp.int32).reshape(1)

    turned = local(turn_body, jax.ShapeDtypeStruct((cols, LAYERS * rows), half))(me, iterate, from_layer(iterate))
    panel = ring(iterate)

    def sums(steps):
        n = len(steps)
        parts = [part for s in steps for part in panel[s]]
        keep, send = local(
            functools.partial(gram_body, [len(panel[s]) for s in steps]),
            (
                jax.ShapeDtypeStruct((n, Y, unit, wide), jnp.float32),
                jax.ShapeDtypeStruct((n, Y, unit, wide), half),
            ),
            [pltpu.VMEM((n * rows, cols), half), pltpu.VMEM((n * rows, rows), jnp.float32)],
            flops=2 * n * rows * wide * cols,
        )(me, *parts, turned)
        return keep, send

    keep, send = sums(GROUPS[0])
    send, *last = lax.optimization_barrier((send, *panel[Z // 2]))
    panel[Z // 2] = tuple(last)
    late, late_send = sums(GROUPS[1])
    first, *rest = local(
        functools.partial(pair_body, GROUPS),
        [jax.ShapeDtypeStruct((Z, unit, wide), jnp.float32)]
        + [jax.ShapeDtypeStruct((Z, unit, wide), half)] * (Y - 1),
    )(me, keep, from_core(send), late, from_core(late_send))
    gram = local(
        functools.partial(finish_body, width),
        jax.ShapeDtypeStruct((Z, unit, wide), half),
    )(me, first, *[from_y(r, -j) for j, r in sorted(enumerate(rest, 1), key=lambda t: t[0] != 2)])

    def column(mine):
        got = [mine] + [from_y(mine, j) for j in range(1, Y)]
        return [piece for g in got for piece in (g, from_core(g))]

    bar = lax.optimization_barrier
    flat = gram.reshape(Z * unit, wide)
    theirs = from_layer(gram)
    mine = [gram] + [from_y(gram, j) for j in range(1, Y)]
    around = {0: (flat,)}
    up, down = from_z(flat, 1), from_z(flat, -1)
    around[1], around[7] = (up,), (down,)
    up, down, theirs = bar((up, down, theirs))
    more = [theirs, from_y(theirs, 1), None, from_y(theirs, 3)]
    up, down = from_z(up, 1), from_z(down, -1)
    around[2], around[6] = (up,), (down,)
    up, down, *mine = bar((up, down, *mine))
    more[2] = from_layer(mine[2])
    mine = [piece for g in mine for piece in (g, from_core(g))]
    up, down = from_z(up, 1), from_z(down, -1)
    around[3], around[5] = (up,), (down,)
    up, down, *more = bar((up, down, *more))
    more = [piece for g in more for piece in (g, from_core(g))]
    around[4] = (from_z(up, 1),)
    poly = local(
        functools.partial(poly_body, [len(around[s]) for s in range(Z)]),
        [jax.ShapeDtypeStruct((Z, unit, rows), half)] * LAYERS,
        [pltpu.VMEM((Z * wide, wide), half)],
        flops=2 * rows * wide * Z * wide,
    )(me, *[part for s in range(Z) for part in around[s]], *mine, *more, gram)

    def column(mine):
        far = from_y(mine, 2)
        got = [mine, from_y(mine, 1), far, from_y(mine, 3)]
        return [piece for g in got for piece in (g, from_core(g))]

    parts = [part for s in range(Z) for part in panel[s]]
    counts = [len(panel[s]) for s in range(Z)]

    def product(pieces, scaled, *more):
        return local(
            functools.partial(apply_body, counts, scaled),
            jax.ShapeDtypeStruct((rows, cols), jnp.float32 if scaled else half),
            [pltpu.VMEM((Z * rows, rows), half)],
            flops=2 * rows * Z * rows * cols,
        )(me, *pieces, *parts, *more)

    add = product(column(poly[1]), False)
    own = poly[0]
    add = from_layer(add)
    mine = product(column(own), True, iterate)
    return (mine + add.astype(jnp.float32)).astype(half)


def solution(mesh):
    return jax.shard_map(
        per_device,
        mesh=mesh,
        in_specs=(P(("wa", "row"), "col"),),
        out_specs=P(("wa", "row"), "col"),
        check_vma=False,
    )
```

```python
import functools

import jax
import jax.numpy as jnp
from jax import lax
from jax.experimental import pallas as pl
from jax.experimental.pallas import tpu as pltpu
from jax.sharding import PartitionSpec as P

coef_first = 3.4445
coef_second = -4.775
coef_third = 2.0315

Z, LAYERS, Y, CORES = 8, 2, 4, 2
UNITS = Y * CORES
GROUPS = ((0, 1, 7, 2, 6, 3, 5), (4,))


def from_z(x, step):
    pairs = [
        (((z + step) % Z) * LAYERS + layer, z * LAYERS + layer)
        for z in range(Z)
        for layer in range(LAYERS)
    ]
    return lax.ppermute(x, "row", pairs)


def from_layer(x):
    return lax.ppermute(x, "row", [(i ^ 1, i) for i in range(Z * LAYERS)])


def from_core(x):
    return lax.ppermute(x, "col", [(i ^ 1, i) for i in range(Y * CORES)])


def from_y(x, step):
    pairs = [
        (((y + step) % Y) * CORES + core, y * CORES + core)
        for y in range(Y)
        for core in range(CORES)
    ]
    return lax.ppermute(x, "col", pairs)


def ring(block, chunks=2):
    size = block.shape[0] // chunks
    up = [block[i * size : (i + 1) * size] for i in range(chunks)]
    down = list(up)
    got = {0: (block,)}
    for step in range(1, Z // 2):
        for i in range(chunks):
            up[i], down[i] = from_z(up[i], 1), from_z(down[i], -1)
        got[step], got[Z - step] = tuple(up), tuple(down)
    half = block.shape[0] // 2
    if chunks == 1:
        got[Z // 2] = (from_z(up[0][:half], 1), from_z(down[0][half:], -1))
    else:
        lower = tuple(from_z(p, 1) for p in up[: chunks // 2])
        got[Z // 2] = lower + tuple(from_z(p, -1) for p in down[chunks // 2 :])
    return got


def nt(left, right):
    return lax.dot_general(
        left, right, (((1,), (1,)), ((), ())), preferred_element_type=jnp.float32
    )


def tn(left, right):
    return lax.dot_general(
        left, right, (((0,), (0,)), ((), ())), preferred_element_type=jnp.float32
    )


def local(body, out, scratch=(), flops=0):
    def call(*args):
        moved = sum(a.size * a.dtype.itemsize for a in args)
        return pl.pallas_call(
            body,
            out_shape=out,
            in_specs=[pl.BlockSpec(memory_space=pltpu.SMEM)]
            + [pl.BlockSpec(memory_space=pltpu.VMEM) for _ in args[1:]],
            out_specs=jax.tree.map(lambda _: pl.BlockSpec(memory_space=pltpu.VMEM), out),
            scratch_shapes=list(scratch),
            compiler_params=pltpu.CompilerParams(vmem_limit_bytes=16 * 2**20),
            cost_estimate=pl.CostEstimate(flops=flops, bytes_accessed=moved, transcendentals=0),
        )(*args)

    return call


def place(me, i):
    j, e = i // CORES, i % CORES
    y, core = me // CORES, me % CORES
    core = 1 - core if e else core
    return (y + j) % Y * CORES + core


def turn_body(me, own, other, out):
    rows = own.shape[0]
    out[:, :rows] = own[...].T
    out[:, rows:] = other[...].T


def gram_body(counts, me, *refs):
    blocks, (turned, keep, send, stack, term) = refs[: sum(counts)], refs[sum(counts) :]
    rows = turned.shape[1] // LAYERS
    unit = rows // UNITS
    start = 0
    for ref in blocks:
        stack[start : start + ref.shape[0], :] = ref[...]
        start += ref.shape[0]
    for layer in range(LAYERS):
        cols = slice(layer * rows, (layer + 1) * rows)
        term[...] = jnp.dot(stack[...], turned[:, cols], preferred_element_type=jnp.float32)
        for b in range(len(counts)):
            for u in range(UNITS):
                piece = term[pl.ds(b * rows + place(me[0], u) * unit, unit), :]
                if u % CORES == 0:
                    keep[b, u // CORES, :, cols] = piece
                else:
                    send[b, u // CORES, :, cols] = piece.astype(send.dtype)


def pair_body(groups, me, *refs):
    ins, (first, *rest) = refs[: 2 * len(groups)], refs[2 * len(groups) :]
    for g, steps in enumerate(groups):
        keep, got = ins[2 * g], ins[2 * g + 1]
        for i, s in enumerate(steps):
            first[s] = keep[i, 0] + got[i, 0].astype(jnp.float32)
            for j in range(1, Y):
                rest[j - 1][s] = (keep[i, j] + got[i, j].astype(jnp.float32)).astype(rest[j - 1].dtype)


def finish_body(width, me, first, *refs):
    rest, gram = refs[:-1], refs[-1]
    total = first[...]
    for r in rest:
        total = total + r[...].astype(jnp.float32)
    gram[...] = (total / width).astype(gram.dtype)


def poly_body(counts, me, *refs):
    around, refs = refs[: sum(counts)], refs[sum(counts) :]
    mine, theirs, (gram, *outs, down) = refs[:UNITS], refs[UNITS : 2 * UNITS], refs[2 * UNITS :]
    unit, wide = gram.shape[1], gram.shape[2]
    rows = wide // LAYERS
    for s in range(Z):
        for u in range(UNITS):
            at = s * wide + place(me[0], u) * unit
            down[pl.ds(at, unit), :] = mine[u][s]
            down[pl.ds(at + rows, unit), :rows] = theirs[u][s, :, rows:]
            down[pl.ds(at + rows, unit), rows:] = theirs[u][s, :, :rows]
    total = coef_second * gram[...].reshape(Z * unit, wide).astype(jnp.float32)
    for s in range(Z):
        parts = [r[...] for r in around[sum(counts[:s]) : sum(counts[: s + 1])]]
        block = parts[0] if len(parts) == 1 else jnp.concatenate(parts, axis=0)
        part = jnp.dot(block, down[s * wide : (s + 1) * wide, :], preferred_element_type=jnp.float32)
        if s:
            cut = (Z - s) * unit
            part = jnp.concatenate([part[cut:], part[:cut]], axis=0)
        total = total + coef_third * part
    for layer, out in enumerate(outs):
        half = total[:, layer * rows : (layer + 1) * rows]
        out[...] = half.astype(out.dtype).reshape(Z, unit, rows)


def apply_body(counts, scaled, cols, me, *refs):
    pieces, refs = refs[:UNITS], refs[UNITS:]
    panel, refs = refs[: sum(counts)], refs[sum(counts) :]
    poly, out = refs[-1], refs[-2]
    unit, rows = pieces[0].shape[1], pieces[0].shape[2]
    for s in range(Z):
        for u in range(UNITS):
            poly[pl.ds(s * rows + place(me[0], u) * unit, unit), :] = pieces[u][s]
    total = None
    for s in range(Z):
        parts = [r[:, cols] for r in panel[sum(counts[:s]) : sum(counts[: s + 1])]]
        block = parts[0] if len(parts) == 1 else jnp.concatenate(parts, axis=0)
        term = tn(poly[s * rows : (s + 1) * rows, :], block)
        total = term if total is None else total + term
    if scaled:
        total = coef_first * refs[0][...].astype(jnp.float32) + total
    out[...] = total.astype(out.dtype)


def add_body(me, mine, first, second, out):
    cut = first.shape[1]
    out[:, :cut] = (mine[:, :cut] + first[...].astype(jnp.float32)).astype(out.dtype)
    out[:, cut:] = (mine[:, cut:] + second[...].astype(jnp.float32)).astype(out.dtype)


def per_device(iterate):
    rows, cols = iterate.shape
    unit = rows // UNITS
    width = cols * lax.axis_size("col")
    wide = LAYERS * rows
    half = jnp.bfloat16
    me = lax.axis_index("col").astype(jnp.int32).reshape(1)

    turned = local(turn_body, jax.ShapeDtypeStruct((cols, LAYERS * rows), half))(me, iterate, from_layer(iterate))
    panel = ring(iterate)

    def sums(steps):
        n = len(steps)
        parts = [part for s in steps for part in panel[s]]
        keep, send = local(
            functools.partial(gram_body, [len(panel[s]) for s in steps]),
            (
                jax.ShapeDtypeStruct((n, Y, unit, wide), jnp.float32),
                jax.ShapeDtypeStruct((n, Y, unit, wide), half),
            ),
            [pltpu.VMEM((n * rows, cols), half), pltpu.VMEM((n * rows, rows), jnp.float32)],
            flops=2 * n * rows * wide * cols,
        )(me, *parts, turned)
        return keep, send

    keep, send = sums(GROUPS[0])
    send, *last = lax.optimization_barrier((send, *panel[Z // 2]))
    panel[Z // 2] = tuple(last)
    late, late_send = sums(GROUPS[1])
    first, *rest = local(
        functools.partial(pair_body, GROUPS),
        [jax.ShapeDtypeStruct((Z, unit, wide), jnp.float32)]
        + [jax.ShapeDtypeStruct((Z, unit, wide), half)] * (Y - 1),
    )(me, keep, from_core(send), late, from_core(late_send))
    gram = local(
        functools.partial(finish_body, width),
        jax.ShapeDtypeStruct((Z, unit, wide), half),
    )(me, first, *[from_y(r, -j) for j, r in sorted(enumerate(rest, 1), key=lambda t: t[0] != 2)])

    def column(mine):
        got = [mine] + [from_y(mine, j) for j in range(1, Y)]
        return [piece for g in got for piece in (g, from_core(g))]

    bar = lax.optimization_barrier
    flat = gram.reshape(Z * unit, wide)
    theirs = from_layer(gram)
    mine = [gram] + [from_y(gram, j) for j in range(1, Y)]
    around = {0: (flat,)}
    up, down = from_z(flat, 1), from_z(flat, -1)
    around[1], around[7] = (up,), (down,)
    up, down, theirs = bar((up, down, theirs))
    more = [theirs, from_y(theirs, 1), None, from_y(theirs, 3)]
    up, down = from_z(up, 1), from_z(down, -1)
    around[2], around[6] = (up,), (down,)
    up, down, *mine = bar((up, down, *mine))
    more[2] = from_layer(mine[2])
    mine = [piece for g in mine for piece in (g, from_core(g))]
    up, down = from_z(up, 1), from_z(down, -1)
    around[3], around[5] = (up,), (down,)
    up, down, *more = bar((up, down, *more))
    more = [piece for g in more for piece in (g, from_core(g))]
    around[4] = (from_z(up, 1),)
    poly = local(
        functools.partial(poly_body, [len(around[s]) for s in range(Z)]),
        [jax.ShapeDtypeStruct((Z, unit, rows), half)] * LAYERS,
        [pltpu.VMEM((Z * wide, wide), half)],
        flops=2 * rows * wide * Z * wide,
    )(me, *[part for s in range(Z) for part in around[s]], *mine, *more, gram)

    def column(mine):
        far = from_y(mine, 2)
        got = [mine, from_y(mine, 1), far, from_y(mine, 3)]
        return [piece for g in got for piece in (g, from_core(g))]

    parts = [part for s in range(Z) for part in panel[s]]
    counts = [len(panel[s]) for s in range(Z)]

    def product(pieces, scaled, at, *more):
        return local(
            functools.partial(apply_body, counts, scaled, at),
            jax.ShapeDtypeStruct((rows, at.stop - at.start), jnp.float32 if scaled else half),
            [pltpu.VMEM((Z * rows, rows), half)],
            flops=2 * rows * Z * rows * (at.stop - at.start),
        )(me, *pieces, *parts, *more)

    there = column(poly[1])
    cut = cols // 256 * 128 + 128
    add = [from_layer(product(there, False, at)) for at in (slice(0, cut), slice(cut, cols))]
    mine = product(column(poly[0]), True, slice(0, cols), iterate)
    return local(add_body, jax.ShapeDtypeStruct((rows, cols), half))(me, mine, *add)


def solution(mesh):
    return jax.shard_map(
        per_device,
        mesh=mesh,
        in_specs=(P(("wa", "row"), "col"),),
        out_specs=P(("wa", "row"), "col"),
        check_vma=False,
    )
```
